32 devices in a mesh: dp: 16 (over z, x, core), mp: 2 (over y).
Axes of the slice: x: 2, y: 2, z: 4, core: 2. Of those that a mesh axis runs over, the one named last changes fastest.
Arguments:
- tokens: bfloat16 [16, 1024, 3584], P('dp'), may hold values from -14 to 14
- modality: int32 [16, 8], P('dp'), may hold values from 0 to 1, as said below
- block_mask: int32 [16, 8, 8], P('dp'), may hold values from 0 to 2, as said below
- q_weight: bfloat16 [2, 3584, 2048], P(None, 'dp', 'mp'), may hold values from -0.09375 to 0.09375
- kv_weight: bfloat16 [2, 3584, 1024], P(None, 'dp'), may hold values from -0.09375 to 0.09375
- o_weight: bfloat16 [2, 2048, 3584], P(None, 'mp', 'dp'), may hold values from -0.125 to 0.125
Outputs:
- attn_out: bfloat16 [16, 1024, 3584], P('dp', 'mp')
The draws below stay inside these ranges and needn't reach their ends.
Inputs may be any that keep to these rules, and one draw needn't show every extreme that they name: modality[s, b] names the section (0 text, 1 image) whose weights serve the 128 tokens of block b of sequence s. block_mask[s, i, j] tells which tokens of block i see block j: 0 none, 1 all, 2 those at or before the query's position; every diagonal entry is 1 or 2, every entry off the diagonal is 0 or 1.
All inputs are finite; a program needn't handle non-finite values.
Results may differ from the reference program's by a relative error of at most 0.015.
Values may be sent and summed in bfloat16 or wider, within the bound.
A program may use at most 128 MiB of HBM per device.

```python
import jax
import jax.numpy as jnp
from jax import lax

D = 3584
HD = 128
KVH = 4
QHEADS = 16
BLK = 128
SEQ = 1024
SEQS = 16
NBLK = 8
N_MP = 2


def sequence_layout(key):
    subkeys = jax.random.split(key, 4)
    block_place = jnp.arange(NBLK, dtype=jnp.int32)
    doc_rate = jax.random.randint(subkeys[0], (), 1, NBLK + 1)
    doc_start = (jax.random.randint(subkeys[1], (NBLK,), 0, 4 * NBLK) < doc_rate) | (block_place == 0)
    run_start = doc_start | (jax.random.randint(subkeys[2], (NBLK,), 0, 3) == 0)
    doc_id = jnp.cumsum(doc_start.astype(jnp.int32)) - 1
    run_id = jnp.cumsum(run_start.astype(jnp.int32)) - 1
    run_kind = jax.random.randint(subkeys[3], (NBLK,), 0, 2)
    block_kinds = run_kind[run_id].astype(jnp.int32)
    row_index = block_place[:, None]
    col_index = block_place[None, :]
    same_doc = doc_id[:, None] == doc_id[None, :]
    lower_ok = (col_index < row_index) & same_doc
    upper_ok = (col_index > row_index) & (run_id[:, None] == run_id[None, :]) & (block_kinds[:, None] == 1)
    diag_value = jnp.where(block_kinds == 1, 1, 2).astype(jnp.int32)
    mask_table = jnp.where(row_index == col_index, diag_value[:, None], jnp.where(lower_ok | upper_ok, 1, 0))
    return (block_kinds, mask_table.astype(jnp.int32))


def all_layouts(key):
    return jax.vmap(sequence_layout)(jax.random.split(jax.random.fold_in(key, 17), SEQS))


def draw_modality(key, part):
    return all_layouts(key)[0]


def draw_block_mask(key, part):
    return all_layouts(key)[1]


def draw_tokens(key, part):
    drawn = jnp.clip(jax.random.normal(key, (SEQS, SEQ, D), jnp.float32), -6.0, 6.0)
    return drawn.astype(jnp.bfloat16)


def block_scale(key, dims, cuts, smallest, top_value):
    factor_of = 1.0
    for dim, parts in cuts:
        heights = jax.random.uniform(jax.random.fold_in(jax.random.fold_in(key, 6), dim), (parts,), jnp.float32, smallest / len(cuts), top_value / len(cuts))
        factor_of = factor_of * jnp.repeat(jnp.exp(heights), dims[dim] // parts).reshape((-1,) + (1,) * (len(dims) - 1 - dim))
    return factor_of


def noise(stream_key, extent, scale, limit, shards=(), kind=jnp.bfloat16):
    values = scale * jax.random.normal(stream_key, extent, jnp.float32)
    if shards:
        values = values * block_scale(stream_key, extent, shards, -0.22, 0.18)
    return jnp.clip(values, -limit, limit).astype(kind)


def setup_inputs(seed: int = 0) -> dict:
    key_list = jax.random.split(jax.random.key(seed), 7)
    return {
        "tokens": draw_tokens(jax.random.fold_in(key_list[6], 71), 0),
        "modality": draw_modality(jax.random.fold_in(key_list[6], 71), 0),
        "block_mask": draw_block_mask(jax.random.fold_in(key_list[6], 71), 0),
        "q_weight": noise(key_list[3], (2, D, QHEADS * HD), D ** -0.5, 0.09375, ((1, 16), (2, 2))),
        "kv_weight": noise(key_list[4], (2, D, 2 * KVH * HD), D ** -0.5, 0.09375, ((1, 16),)),
        "o_weight": noise(key_list[5], (2, QHEADS * HD, D), (QHEADS * HD) ** -0.5, 0.125, ((1, 2), (2, 16))),
    }


rope_theta = 1000000.0


def rotary_tables(length, head_width):
    half_width = head_width // 2
    frequency = rope_theta ** (-jnp.arange(half_width, dtype=jnp.float32) * 2.0 / head_width)
    angles = jnp.arange(length, dtype=jnp.float32)[:, None] * frequency[None, :]
    angles = jnp.concatenate([angles, angles], axis=1)
    return jnp.cos(angles), jnp.sin(angles)


def rotate(values, cosine_table, sine_table):
    half_width = values.shape[-1] // 2
    turned = jnp.concatenate([-values[..., half_width:], values[..., :half_width]], axis=-1)
    return values * cosine_table[:, None, :] + turned * sine_table[:, None, :]


def allowed_pairs(layout, first_row, block_rows, length):
    block_count = length // BLK
    rows_mask = lax.dynamic_slice_in_dim(layout, first_row // BLK, block_rows // BLK, 0)
    expanded = jnp.broadcast_to(rows_mask[:, None, :, None], (block_rows // BLK, BLK, block_count, BLK)).reshape(block_rows, length)
    positions = jnp.arange(length, dtype=jnp.int32)
    query_pos = first_row + jnp.arange(block_rows, dtype=jnp.int32)
    return (expanded == 1) | ((expanded == 2) & (positions[None, :] <= query_pos[:, None]))


def reference(tokens, modality, block_mask, q_weight, kv_weight, o_weight):
    group_size = QHEADS // KVH
    block_rows = min(512, SEQ)
    cosine_table, sine_table = rotary_tables(SEQ, HD)
    score_scale = HD ** -0.5
    group_cols = QHEADS * HD // N_MP

    def one_sequence(inputs):
        states, block_kinds, layout = inputs
        blocks = states.reshape(NBLK, BLK, D)

        def project(pieces):
            row_block, block_kind = pieces
            query_weight = lax.dynamic_index_in_dim(q_weight, block_kind, 0, keepdims=False)
            pair_weight = lax.dynamic_index_in_dim(kv_weight, block_kind, 0, keepdims=False)
            return (jnp.dot(row_block, query_weight, preferred_element_type=jnp.float32),
                    jnp.dot(row_block, pair_weight, preferred_element_type=jnp.float32))

        query_raw, pair_raw = lax.map(project, (blocks, block_kinds))
        queries = rotate(query_raw.reshape(SEQ, QHEADS, HD), cosine_table, sine_table)
        queries = queries.astype(jnp.bfloat16).reshape(SEQ, KVH, group_size, HD)
        pairs = pair_raw.reshape(SEQ, KVH, 2, HD)
        key_heads = rotate(pairs[:, :, 0], cosine_table, sine_table).astype(jnp.bfloat16)
        value_heads = pairs[:, :, 1].astype(jnp.bfloat16)

        def attend(block_index):
            first_row = block_index * block_rows
            query_part = lax.dynamic_slice_in_dim(queries, first_row, block_rows, 0)
            allowed = allowed_pairs(layout, first_row, block_rows, SEQ)
            scores = jnp.einsum("qgjd,kgd->gjqk", query_part.astype(jnp.float32), key_heads.astype(jnp.float32)) * score_scale
            scores = jnp.where(allowed[None, None], scores, -1e30)
            row_max = jnp.max(scores, axis=-1, keepdims=True)
            weights = jnp.exp(scores - row_max)
            weights = (weights / jnp.sum(weights, axis=-1, keepdims=True)).astype(jnp.bfloat16)
            mixed_out = jnp.einsum("gjqk,kgd->qgjd", weights.astype(jnp.float32), value_heads.astype(jnp.float32))
            return mixed_out.astype(jnp.bfloat16).reshape(block_rows, QHEADS * HD)

        attended = lax.map(attend, jnp.arange(SEQ // block_rows, dtype=jnp.int32))
        attended = attended.reshape(NBLK, BLK, N_MP, group_cols)

        def finish(pieces):
            row_block, block_kind = pieces
            out_weight = lax.dynamic_index_in_dim(o_weight, block_kind, 0, keepdims=False).reshape(N_MP, group_cols, D)
            group_parts = jnp.einsum("kgc,gcd->gkd", row_block.astype(jnp.float32), out_weight.astype(jnp.float32))
            group_parts = lax.optimization_barrier(group_parts.astype(jnp.bfloat16)).astype(jnp.float32)
            return jnp.sum(group_parts, axis=0).astype(jnp.bfloat16)

        return lax.map(finish, (attended, block_kinds)).reshape(SEQ, D)

    return lax.map(one_sequence, (tokens, modality, block_mask))
```

```python
import functools
import math

import jax
import jax.numpy as jnp
import numpy as np
from jax import lax
from jax.experimental import pallas as pl
from jax.experimental.pallas import tpu as pltpu
from jax.sharding import PartitionSpec as P

HD = 128
KVH = 4
QHEADS = 16
BLK = 128
CORES = 2
MESH = pl.DeviceIdType.MESH
NT = (((1,), (1,)), ((), ()))


rope_theta = 1000000.0


def rotary_tables(length, head_width):
    half_width = head_width // 2
    frequency = rope_theta ** (-np.arange(half_width, dtype=np.float32) * 2.0 / head_width)
    angles = np.arange(length, dtype=np.float32)[:, None] * frequency.astype(np.float32)[None, :]
    sines = np.sin(angles)
    return (
        np.concatenate([np.cos(angles)] * 2, axis=1).astype(np.float32),
        np.concatenate([-sines, sines], axis=1).astype(np.float32),
    )


def split_chips(devices):
    chips = devices // CORES
    inner = 1 << (int(math.log2(chips)) // 2)
    return chips // inner, inner


def kernel(
    lines, inner, mps, heads, pairs,
    tok, in_qkv, in_o, kinds, layout, cosine, sine,
    out,
    w_qkv, w_o, acc, queries, keys, values, tok_stage, send_buf, recv_buf, out_stage,
    load_sem, z_sem, x_sem, core_sem, recv_sem, y_send, y_recv, tok_sem, out_sem,
):
    length, width = tok.shape
    plane_cols = width // lines
    slots, shard_rows = w_qkv.shape[2], w_qkv.shape[3]
    part_rows = length // mps
    q_cols = heads * HD
    per_pair = heads // pairs
    row_tile = min(512, length)
    out_tile = min(256, part_rows)

    me = lax.axis_index("dp")
    mp = lax.axis_index("mp")
    core = me % CORES
    x = (me // CORES) % inner
    z = me // (CORES * inner)
    other = 1 - core
    mine = x * CORES + core

    def at(z_, x_, core_):
        return ((z_ * inner + x_) * CORES + core_, mp)

    def order(k):
        picked = jnp.int32(0)
        for place in range(lines):
            ranked = sorted(range(lines), key=lambda p: (abs(p - place), p))
            picked = jnp.where(z == place, ranked[k], picked)
        return picked

    weights = (w_qkv, w_o)

    def send(ph, p, s, m, sem, device):
        block = weights[ph].at[p, m, s]
        return pltpu.make_async_remote_copy(
            src_ref=block, dst_ref=block, send_sem=sem, recv_sem=recv_sem.at[ph, p, s, m],
            device_id=device, device_id_type=MESH,
        )

    def z_copies(ph, p, m):
        up = send(ph, p, mine, m, z_sem.at[ph, 0, p, m], at(z + 1, x, core))
        down = send(ph, p, mine, m, z_sem.at[ph, 1, p, m], at(z - 1, x, core))
        return ((p <= z) & (z < lines - 1), up), ((p >= z) & (z > 0), down)

    def push_z(ph, p, m):
        for condition, copy in z_copies(ph, p, m):
            pl.when(condition)(copy.start)

    def x_copy(ph, p, j, m):
        return send(ph, p, mine, m, x_sem.at[ph, j - 1, p, m], at(z, (x + j) % inner, core))

    def core_copy(ph, p, j, m):
        slot = ((x + j) % inner) * CORES + core
        return send(ph, p, slot, m, core_sem.at[ph, j, p, m], at(z, x, other))

    def push_xc(ph, p, m):
        for j in range(1, inner):
            x_copy(ph, p, j, m).start()
        core_copy(ph, p, 0, m).start()

    def arrived(ph, p, s, m):
        send(ph, p, s, m, core_sem.at[ph, 0, p, m], at(z, x, other)).wait_recv()

    def lane(ph, distance):
        for m in range(2):
            for valid, p in ((z >= distance, z - distance), (z + distance < lines, z + distance)):
                @pl.when(valid)
                def _():
                    arrived(ph, p, mine, m)
                    push_z(ph, p, m)
                    push_xc(ph, p, m)

    def complete(ph, p):
        for m in range(2):
            for j in range(1, inner):
                arrived(ph, p, ((x + j) % inner) * CORES + core, m)
                core_copy(ph, p, j, m).start()
        for m in range(2):
            for j in range(inner):
                arrived(ph, p, j * CORES + other, m)

    def token_copy(k):
        columns = pl.ds(pl.multiple_of(order(k) * plane_cols, 128), plane_cols)
        return pltpu.make_async_copy(tok.at[:, columns], tok_stage, tok_sem.at[k])

    def project(k):
        p = order(k)
        token_copy(k).wait()
        col_tile = min(512, w_qkv.shape[4])
        for c in range(0, w_qkv.shape[4], col_tile):
            @pl.loop(0, length // row_tile)
            def _(i):
                rows = pl.ds(pl.multiple_of(i * row_tile, row_tile), row_tile)
                block = tok_stage[rows, :]
                text = w_qkv[p, 0, :, :, c : c + col_tile].reshape(plane_cols, col_tile)
                image = w_qkv[p, 1, :, :, c : c + col_tile].reshape(plane_cols, col_tile)
                result = jnp.where(
                    kinds[rows, :] == 1,
                    jnp.dot(block, image, preferred_element_type=jnp.float32),
                    jnp.dot(block, text, preferred_element_type=jnp.float32),
                )
                if k == 0:
                    acc[rows, c : c + col_tile] = result
                else:
                    acc[rows, c : c + col_tile] += result
        if k + 1 < lines:
            token_copy(k + 1).start()

    def rope():
        tile = min(256, length)

        @pl.loop(0, length // tile)
        def _(i):
            rows = pl.ds(pl.multiple_of(i * tile, tile), tile)
            cos, sin = cosine[rows, :], sine[rows, :]

            def turned(first):
                part = acc[rows, first : first + HD]
                return (part * cos + pltpu.roll(part, HD // 2, 1) * sin).astype(jnp.bfloat16)

            for h in range(heads):
                queries[rows, h * HD : (h + 1) * HD] = turned(h * HD)
            for g in range(pairs):
                first = q_cols + g * 2 * HD
                keys[rows, g * HD : (g + 1) * HD] = turned(first)
                values[rows, g * HD : (g + 1) * HD] = acc[rows, first + HD : first + 2 * HD].astype(
                    jnp.bfloat16
                )

    def attend(part):
        scale = HD ** (-0.5)
        together = 2 if per_pair % 2 == 0 else 1

        @pl.loop(0, part_rows // BLK)
        def _(i):
            block = part * (part_rows // BLK) + i
            rows = pl.ds(pl.multiple_of(block * BLK, BLK), BLK)
            seen = layout[pl.ds(block, 1), :]
            key_pos = lax.broadcasted_iota(jnp.int32, (BLK, length), 1)
            query_pos = lax.broadcasted_iota(jnp.int32, (BLK, length), 0) + block * BLK
            last = jnp.where(seen == 1, length, jnp.where(seen == 2, 0, -length))
            bias = jnp.where(key_pos <= query_pos + last, 0.0, -1e30)
            for g in range(pairs):
                key, value = keys[:, g * HD : (g + 1) * HD], values[:, g * HD : (g + 1) * HD]
                for first in range(g * per_pair, (g + 1) * per_pair, together):
                    query = jnp.concatenate(
                        [queries[rows, h * HD : (h + 1) * HD] for h in range(first, first + together)],
                        axis=0,
                    )
                    scores = lax.dot_general(query, key, NT, preferred_element_type=jnp.float32)
                    scores = scores.reshape(together, BLK, length) * scale + bias[None]
                    share = jnp.exp(scores - jnp.max(scores, axis=-1, keepdims=True))
                    total = jnp.sum(share, axis=-1, keepdims=True)
                    mixed = jnp.dot(
                        share.astype(jnp.bfloat16).reshape(together * BLK, length),
                        value,
                        preferred_element_type=jnp.float32,
                    ).reshape(together, BLK, HD) / total
                    for h in range(together):
                        queries[rows, (first + h) * HD : (first + h + 1) * HD] = mixed[h].astype(
                            jnp.bfloat16
                        )

    def out_rows(p, first, store):
        @pl.loop(0, part_rows // out_tile)
        def _(i):
            rows = pl.ds(pl.multiple_of(first + i * out_tile, out_tile), out_tile)
            block = queries[rows, :]
            text = w_o[p, 0].reshape(plane_cols, q_cols)
            image = w_o[p, 1].reshape(plane_cols, q_cols)
            result = jnp.where(
                kinds[rows, :] == 1,
                lax.dot_general(block, image, NT, preferred_element_type=jnp.float32),
                lax.dot_general(block, text, NT, preferred_element_type=jnp.float32),
            )
            store(pl.ds(pl.multiple_of(i * out_tile, out_tile), out_tile), result.astype(jnp.bfloat16))

    def y_copy(k, j):
        return pltpu.make_async_remote_copy(
            src_ref=send_buf.at[k, j - 1], dst_ref=recv_buf.at[k, j - 1],
            send_sem=y_send.at[k, j - 1], recv_sem=y_recv.at[k, j - 1],
            device_id=(me, (mp + j) % mps), device_id_type=MESH,
        )

    def give(k):
        for j in range(1, mps):
            def store(rows, result):
                send_buf[k, j - 1, rows, :] = result

            out_rows(order(k), ((mp + j) % mps) * part_rows, store)
            y_copy(k, j).start()

    def out_copy(k):
        columns = pl.ds(pl.multiple_of(order(k) * plane_cols, 128), plane_cols)
        return pltpu.make_async_copy(out_stage.at[k % 2], out.at[:, columns], out_sem.at[k])

    def take(k):
        if k >= 2:
            out_copy(k - 2).wait()
        for j in range(1, mps):
            y_copy(k, j).wait_recv()

        def store(rows, result):
            total = result.astype(jnp.float32)
            for j in range(1, mps):
                total += recv_buf[k, j - 1, rows, :].astype(jnp.float32)
            out_stage[k % 2, rows, :] = total.astype(jnp.bfloat16)

        out_rows(order(k), mp * part_rows, store)
        out_copy(k).start()

    loads = [
        pltpu.make_async_copy(source, target.at[z, :, mine], load_sem.at[i])
        for i, (source, target) in enumerate(((in_qkv, w_qkv), (in_o, w_o)))
    ]
    for load in loads:
        load.start()
    token_copy(0).start()

    barrier = pltpu.get_barrier_semaphore()

    def greet(device):
        pl.semaphore_signal(barrier, inc=1, device_id=device, device_id_type=MESH)

    pl.when(z > 0)(lambda: greet(at(z - 1, x, core)))
    pl.when(z < lines - 1)(lambda: greet(at(z + 1, x, core)))
    for j in range(1, inner):
        greet(at(z, (x + j) % inner, core))
    greet(at(z, x, other))
    for j in range(1, mps):
        greet((me, (mp + j) % mps))
    ends = jnp.where(z > 0, 1, 0) + jnp.where(z < lines - 1, 1, 0)
    pl.semaphore_wait(barrier, inner + mps - 1 + ends)

    loads[0].wait()
    for m in range(2):
        push_z(0, z, m)
        push_xc(0, z, m)
    loads[1].wait()
    for k in range(lines):
        if k + 1 < lines:
            lane(0, k + 1)
        if k == max(lines - 2, 0):
            for m in range(2):
                push_z(1, z, m)
        complete(0, order(k))
        if k == lines - 1:
            for m in range(2):
                push_xc(1, z, m)
        project(k)
    if lines > 1:
        lane(1, 1)
    rope()
    for j in range(1, mps):
        attend((mp + j) % mps)
    if lines > 2:
        lane(1, 2)
    complete(1, order(0))
    give(0)
    attend(mp)
    for distance in range(3, lines):
        lane(1, distance)
    for k in range(1, lines):
        complete(1, order(k))
        give(k)
        take(k - 1)
    take(lines - 1)

    for k in range(max(lines - 2, 0), lines):
        out_copy(k).wait()
    for k in range(lines):
        for j in range(1, mps):
            y_copy(k, j).wait_send()
    for ph in range(2):
        for p in range(lines):
            for m in range(2):
                for condition, copy in z_copies(ph, p, m):
                    pl.when(condition)(copy.wait_send)
                for j in range(1, inner):
                    x_copy(ph, p, j, m).wait_send()
                for j in range(inner):
                    core_copy(ph, p, j, m).wait_send()


def local(devices, mps, tokens, modality, block_mask, q_weight, kv_weight, o_weight):
    states = tokens[0]
    length, width = states.shape
    heads = q_weight.shape[2] // HD
    group_size = QHEADS // KVH
    pairs = max(1, heads // group_size)
    first_pair = lax.axis_index("mp") * heads // group_size
    kv_needed = lax.dynamic_slice_in_dim(kv_weight, first_pair * (2 * HD), pairs * 2 * HD, 2)
    qkv = jnp.concatenate([q_weight, kv_needed], axis=2)
    o_turned = jnp.swapaxes(o_weight, 1, 2)
    kinds = jnp.repeat(modality[0], BLK)[:, None]
    layout = jnp.repeat(block_mask[0], BLK, axis=1)
    cosine, sine = rotary_tables(length, HD)

    lines, inner = split_chips(devices)
    slots = inner * CORES
    plane_cols = width // lines
    part_rows = length // mps
    shard_rows, qkv_cols = qkv.shape[1:]
    bf16, f32 = jnp.bfloat16, jnp.float32
    dma = pltpu.SemaphoreType.DMA
    in_hbm = pl.BlockSpec(memory_space=pltpu.HBM)
    in_vmem = pl.BlockSpec(memory_space=pltpu.VMEM)
    out = pl.pallas_call(
        functools.partial(kernel, lines, inner, mps, heads, pairs),
        out_shape=jax.ShapeDtypeStruct((part_rows, width), bf16),
        in_specs=[in_hbm] * 3 + [in_vmem] * 4,
        out_specs=in_hbm,
        scratch_shapes=[
            pltpu.VMEM((lines, 2, slots, shard_rows, qkv_cols), bf16),
            pltpu.VMEM((lines, 2, slots, shard_rows, heads * HD), bf16),
            pltpu.VMEM((length, qkv_cols), f32),
            pltpu.VMEM((length, heads * HD), bf16),
            pltpu.VMEM((length, pairs * HD), bf16),
            pltpu.VMEM((length, pairs * HD), bf16),
            pltpu.VMEM((length, plane_cols), bf16),
            pltpu.VMEM((lines, mps - 1, part_rows, plane_cols), bf16),
            pltpu.VMEM((lines, mps - 1, part_rows, plane_cols), bf16),
            pltpu.VMEM((2, part_rows, plane_cols), bf16),
            dma((2,)),
            dma((2, 2, lines, 2)),
            dma((2, max(inner - 1, 1), lines, 2)),
            dma((2, inner, lines, 2)),
            dma((2, lines, slots, 2)),
            dma((lines, mps - 1)),
            dma((lines, mps - 1)),
            dma((lines,)),
            dma((lines,)),
        ],
        compiler_params=pltpu.CompilerParams(
            collective_id=0, has_side_effects=True, vmem_limit_bytes=64 * 2**20 - 2**19
        ),
        cost_estimate=pl.CostEstimate(
            flops=4 * length * width * (qkv_cols + heads * HD) + 4 * length * length * heads * HD,
            bytes_accessed=4 * length * width,
            transcendentals=length * length * heads,
        ),
    )(states, qkv, o_turned, kinds, layout, cosine, sine)
    return out[None]


def solution(mesh):
    in_specs = (
        P("dp", None, None),
        P("dp", None),
        P("dp", None, None),
        P(None, "dp", "mp"),
        P(None, "dp", None),
        P(None, "mp", "dp"),
    )
    out_specs = P("dp", "mp", None)
    return jax.shard_map(
        functools.partial(local, mesh.shape["dp"], mesh.shape["mp"]),
        mesh=mesh, in_specs=in_specs, out_specs=out_specs, check_vma=False,
    )
```

```python
import functools
import math

import jax
import jax.numpy as jnp
import numpy as np
from jax import lax
from jax.experimental import pallas as pl
from jax.experimental.pallas import tpu as pltpu
from jax.sharding import PartitionSpec as P

HD = 128
KVH = 4
QHEADS = 16
BLK = 128
CORES = 2
MESH = pl.DeviceIdType.MESH
NT = (((1,), (1,)), ((), ()))


rope_theta = 1000000.0


def rotary_tables(length, head_width):
    half_width = head_width // 2
    frequency = rope_theta ** (-np.arange(half_width, dtype=np.float32) * 2.0 / head_width)
    angles = np.arange(length, dtype=np.float32)[:, None] * frequency.astype(np.float32)[None, :]
    sines = np.sin(angles)
    return (
        np.concatenate([np.cos(angles)] * 2, axis=1).astype(np.float32),
        np.concatenate([-sines, sines], axis=1).astype(np.float32),
    )


def split_chips(devices):
    chips = devices // CORES
    inner = 1 << (int(math.log2(chips)) // 2)
    return chips // inner, inner


def kernel(
    lines, inner, mps, heads, pairs,
    tok, in_q, in_kv, in_o, modality, block_mask, cosine, sine,
    out,
    kinds, layout, w_qkv, w_o, acc, queries, keys, values, tok_stage, send_buf, recv_buf, out_stage,
    load_sem, z_sem, x_sem, turn_sem, core_sem, recv_sem, y_send, y_recv, tok_sem, out_sem,
):
    length, width = tok.shape
    plane_cols = width // lines
    slots, shard_rows = w_qkv.shape[2], w_qkv.shape[3]
    part_rows = length // mps
    q_cols = heads * HD
    per_pair = heads // pairs
    row_tile = min(512, length)
    out_tile = min(256, part_rows)

    me = lax.axis_index("dp")
    mp = lax.axis_index("mp")
    core = me % CORES
    x = (me // CORES) % inner
    z = me // (CORES * inner)
    other = 1 - core
    mine = x * CORES + core

    def at(z_, x_, core_):
        return ((z_ * inner + x_) * CORES + core_, mp)

    def order(k):
        picked = jnp.int32(0)
        for place in range(lines):
            ranked = sorted(range(lines), key=lambda p: (abs(p - place), p))
            picked = jnp.where(z == place, ranked[k], picked)
        return picked

    weights = (w_qkv, w_o)

    def send(ph, p, s, m, sem, device):
        block = weights[ph].at[p, m, s]
        return pltpu.make_async_remote_copy(
            src_ref=block, dst_ref=block, send_sem=sem, recv_sem=recv_sem.at[ph, p, s, m],
            device_id=device, device_id_type=MESH,
        )

    def z_copies(ph, p, m):
        up = send(ph, p, mine, m, z_sem.at[ph, 0, p, m], at(z + 1, x, core))
        down = send(ph, p, mine, m, z_sem.at[ph, 1, p, m], at(z - 1, x, core))
        return ((p <= z) & (z < lines - 1), up), ((p >= z) & (z > 0), down)

    def push_z(ph, p, m):
        for condition, copy in z_copies(ph, p, m):
            pl.when(condition)(copy.start)

    def x_copy(ph, p, j, m):
        return send(ph, p, mine, m, x_sem.at[ph, j - 1, p, m], at(z, (x + j) % inner, core))

    def core_copy(ph, p, j, m):
        slot = ((x + j) % inner) * CORES + core
        return send(ph, p, slot, m, core_sem.at[ph, j, p, m], at(z, x, other))

    def ends(p):
        return (p == 0) | (p == lines - 1)

    def takes_x(p, m):
        return (p == z) | jnp.logical_not(ends(p)) if m == 0 else p >= 0

    def push_xc(ph, p, m):
        @pl.when(takes_x(p, m))
        def _():
            for j in range(1, inner):
                x_copy(ph, p, j, m).start()

        core_copy(ph, p, 0, m).start()

    def turn_copies(ph, p, j):
        slot = ((x + j) % inner) * CORES + core
        up = send(ph, p, slot, 0, turn_sem.at[ph, 0, p, j - 1], at(z + 1, x, core))
        down = send(ph, p, slot, 0, turn_sem.at[ph, 1, p, j - 1], at(z - 1, x, core))
        return ((p == 0) & (z < lines - 1), up), ((p == lines - 1) & (z > 0), down)

    def push_turn(ph, p, j):
        for condition, copy in turn_copies(ph, p, j):
            pl.when(condition)(copy.start)

    def turn(ph, distance):
        for valid, p in ((z == distance, 0), (z + distance == lines - 1, lines - 1)):
            @pl.when(valid)
            def _():
                for j in range(1, inner):
                    arrived(ph, p, ((x + j) % inner) * CORES + core, 0)
                    push_turn(ph, p, j)
                    core_copy(ph, p, j, 0).start()

    def arrived(ph, p, s, m):
        send(ph, p, s, m, core_sem.at[ph, 0, p, m], at(z, x, other)).wait_recv()

    def lane(ph, distance):
        for m in range(2):
            for valid, p in ((z >= distance, z - distance), (z + distance < lines, z + distance)):
                @pl.when(valid)
                def _():
                    arrived(ph, p, mine, m)
                    push_z(ph, p, m)
                    push_xc(ph, p, m)

    def complete(ph, p):
        for m in range(2):
            @pl.when(takes_x(p, m))
            def _():
                for j in range(1, inner):
                    arrived(ph, p, ((x + j) % inner) * CORES + core, m)
                    if m == 0:
                        pl.when(p == z)(lambda: push_turn(ph, p, j))
                    core_copy(ph, p, j, m).start()

        for m in range(2):
            for j in range(inner):
                arrived(ph, p, j * CORES + other, m)

    def token_copy(k):
        columns = pl.ds(pl.multiple_of(order(k) * plane_cols, 128), plane_cols)
        return pltpu.make_async_copy(tok.at[:, columns], tok_stage, tok_sem.at[k])

    def project(k):
        p = order(k)
        token_copy(k).wait()
        col_tile = min(512, w_qkv.shape[4])
        for c in range(0, w_qkv.shape[4], col_tile):
            @pl.loop(0, length // row_tile)
            def _(i):
                rows = pl.ds(pl.multiple_of(i * row_tile, row_tile), row_tile)
                block = tok_stage[rows, :]
                text = w_qkv[p, 0, :, :, c : c + col_tile].reshape(plane_cols, col_tile)
                image = w_qkv[p, 1, :, :, c : c + col_tile].reshape(plane_cols, col_tile)
                result = jnp.where(
                    kinds[rows, :] == 1,
                    jnp.dot(block, image, preferred_element_type=jnp.float32),
                    jnp.dot(block, text, preferred_element_type=jnp.float32),
                )
                if k == 0:
                    acc[rows, c : c + col_tile] = result
                else:
                    acc[rows, c : c + col_tile] += result
        if k + 1 < lines:
            token_copy(k + 1).start()

    def rope():
        tile = min(256, length)

        @pl.loop(0, length // tile)
        def _(i):
            rows = pl.ds(pl.multiple_of(i * tile, tile), tile)
            cos, sin = cosine[rows, :], sine[rows, :]

            def turned(first):
                part = acc[rows, first : first + HD]
                return (part * cos + pltpu.roll(part, HD // 2, 1) * sin).astype(jnp.bfloat16)

            for h in range(heads):
                queries[rows, h * HD : (h + 1) * HD] = turned(h * HD)
            for g in range(pairs):
                first = q_cols + g * 2 * HD
                keys[rows, g * HD : (g + 1) * HD] = turned(first)
                values[rows, g * HD : (g + 1) * HD] = acc[rows, first + HD : first + 2 * HD].astype(
                    jnp.bfloat16
                )

    def attend(part, start, stop):
        scale = HD ** (-0.5)
        together = 2 if per_pair % 2 == 0 else 1

        @pl.loop(start, stop)
        def _(i):
            block = part * (part_rows // BLK) + i
            rows = pl.ds(pl.multiple_of(block * BLK, BLK), BLK)
            seen = layout[pl.ds(block, 1), :]
            key_pos = lax.broadcasted_iota(jnp.int32, (BLK, length), 1)
            query_pos = lax.broadcasted_iota(jnp.int32, (BLK, length), 0) + block * BLK
            last = jnp.where(seen == 1, length, jnp.where(seen == 2, 0, -length))
            bias = jnp.where(key_pos <= query_pos + last, 0.0, -1e30)
            for g in range(pairs):
                key, value = keys[:, g * HD : (g + 1) * HD], values[:, g * HD : (g + 1) * HD]
                for first in range(g * per_pair, (g + 1) * per_pair, together):
                    query = jnp.concatenate(
                        [queries[rows, h * HD : (h + 1) * HD] for h in range(first, first + together)],
                        axis=0,
                    )
                    scores = lax.dot_general(query, key, NT, preferred_element_type=jnp.float32)
                    scores = scores.reshape(together, BLK, length) * scale + bias[None]
                    share = jnp.exp(scores - jnp.max(scores, axis=-1, keepdims=True))
                    total = jnp.sum(share, axis=-1, keepdims=True)
                    mixed = jnp.dot(
                        share.astype(jnp.bfloat16).reshape(together * BLK, length),
                        value,
                        preferred_element_type=jnp.float32,
                    ).reshape(together, BLK, HD) / total
                    for h in range(together):
                        queries[rows, (first + h) * HD : (first + h + 1) * HD] = mixed[h].astype(
                            jnp.bfloat16
                        )

    def out_rows(p, first, store):
        @pl.loop(0, part_rows // out_tile)
        def _(i):
            rows = pl.ds(pl.multiple_of(first + i * out_tile, out_tile), out_tile)
            block = queries[rows, :]
            text = w_o[p, 0].reshape(plane_cols, q_cols)
            image = w_o[p, 1].reshape(plane_cols, q_cols)
            result = jnp.where(
                kinds[rows, :] == 1,
                lax.dot_general(block, image, NT, preferred_element_type=jnp.float32),
                lax.dot_general(block, text, NT, preferred_element_type=jnp.float32),
            )
            store(pl.ds(pl.multiple_of(i * out_tile, out_tile), out_tile), result.astype(jnp.bfloat16))

    def y_copy(k, j):
        return pltpu.make_async_remote_copy(
            src_ref=send_buf.at[k, j - 1], dst_ref=recv_buf.at[k, j - 1],
            send_sem=y_send.at[k, j - 1], recv_sem=y_recv.at[k, j - 1],
            device_id=(me, (mp + j) % mps), device_id_type=MESH,
        )

    def give(k):
        for j in range(1, mps):
            def store(rows, result):
                send_buf[k, j - 1, rows, :] = result

            out_rows(order(k), ((mp + j) % mps) * part_rows, store)
            y_copy(k, j).start()

    def out_copy(k):
        columns = pl.ds(pl.multiple_of(order(k) * plane_cols, 128), plane_cols)
        return pltpu.make_async_copy(out_stage.at[k % 2], out.at[:, columns], out_sem.at[k])

    def take(k):
        if k >= 2:
            out_copy(k - 2).wait()
        for j in range(1, mps):
            y_copy(k, j).wait_recv()

        def store(rows, result):
            total = result.astype(jnp.float32)
            for j in range(1, mps):
                total += recv_buf[k, j - 1, rows, :].astype(jnp.float32)
            out_stage[k % 2, rows, :] = total.astype(jnp.bfloat16)

        out_rows(order(k), mp * part_rows, store)
        out_copy(k).start()

    pair_cols = pairs * 2 * HD
    first_pair = (mp * heads // (QHEADS // KVH)) * (2 * HD)
    kv_part = in_kv.at[:, :, pl.ds(pl.multiple_of(first_pair, 2 * HD), pair_cols)]
    loads = [
        pltpu.make_async_copy(in_q, w_qkv.at[z, :, mine, :, pl.ds(0, q_cols)], load_sem.at[0]),
        pltpu.make_async_copy(kv_part, w_qkv.at[z, :, mine, :, pl.ds(q_cols, pair_cols)], load_sem.at[1]),
        pltpu.make_async_copy(in_o, w_o.at[z, :, mine], load_sem.at[2]),
    ]
    for load in loads:
        load.start()
    token_copy(0).start()

    barrier = pltpu.get_barrier_semaphore()

    def greet(device):
        pl.semaphore_signal(barrier, inc=1, device_id=device, device_id_type=MESH)

    pl.when(z > 0)(lambda: greet(at(z - 1, x, core)))
    pl.when(z < lines - 1)(lambda: greet(at(z + 1, x, core)))
    for j in range(1, inner):
        greet(at(z, (x + j) % inner, core))
    greet(at(z, x, other))
    for j in range(1, mps):
        greet((me, (mp + j) % mps))
    along = jnp.where(z > 0, 1, 0) + jnp.where(z < lines - 1, 1, 0)
    pl.semaphore_wait(barrier, inner + mps - 1 + along)

    loads[0].wait()
    loads[1].wait()
    for m in range(2):
        push_z(0, z, m)
        push_xc(0, z, m)
    loads[2].wait()
    blocks = length // BLK
    for i in range(blocks):
        kinds[i * BLK : (i + 1) * BLK, :] = jnp.full((BLK, 1), modality[0, i], jnp.int32)
        for j in range(blocks):
            layout[i : i + 1, j * BLK : (j + 1) * BLK] = jnp.full((1, BLK), block_mask[i, j], jnp.int32)
    for k in range(lines):
        if k > 0:
            turn(0, k)
        if k + 1 < lines:
            lane(0, k + 1)
        if k == max(lines - 2, 0):
            for m in range(2):
                push_z(1, z, m)
        complete(0, order(k))
        if k == lines - 1:
            for m in range(2):
                push_xc(1, z, m)
        project(k)
    if lines > 1:
        lane(1, 1)
    rope()
    part_blocks = part_rows // BLK
    for j in range(1, mps):
        attend((mp + j) % mps, 0, part_blocks)
    complete(1, order(0))
    if lines > 2:
        lane(1, 2)
    give(0)
    attend(mp, 0, part_blocks // 2)
    if lines > 1:
        turn(1, 1)
    attend(mp, part_blocks // 2, part_blocks)
    for k in range(1, lines):
        if k > 1:
            turn(1, k)
        if k + 2 <= lines - 1:
            lane(1, k + 2)
        complete(1, order(k))
        give(k)
        take(k - 1)
    take(lines - 1)

    for k in range(max(lines - 2, 0), lines):
        out_copy(k).wait()
    for k in range(lines):
        for j in range(1, mps):
            y_copy(k, j).wait_send()
    for ph in range(2):
        for p in range(lines):
            for m in range(2):
                for condition, copy in z_copies(ph, p, m):
                    pl.when(condition)(copy.wait_send)
                @pl.when(takes_x(p, m))
                def _():
                    for j in range(1, inner):
                        x_copy(ph, p, j, m).wait_send()

                for j in range(inner):
                    core_copy(ph, p, j, m).wait_send()
            if p in (0, lines - 1):
                for j in range(1, inner):
                    for condition, copy in turn_copies(ph, p, j):
                        pl.when(condition)(copy.wait_send)


def local(devices, mps, tokens, modality, block_mask, q_weight, kv_weight, o_weight):
    states = tokens[0]
    length, width = states.shape
    heads = q_weight.shape[2] // HD
    group_size = QHEADS // KVH
    pairs = max(1, heads // group_size)
    o_turned = jnp.swapaxes(o_weight, 1, 2)
    cosine, sine = rotary_tables(length, HD)

    lines, inner = split_chips(devices)
    slots = inner * CORES
    plane_cols = width // lines
    part_rows = length // mps
    shard_rows, qkv_cols = q_weight.shape[1], (heads + 2 * pairs) * HD
    bf16, f32 = jnp.bfloat16, jnp.float32
    dma = pltpu.SemaphoreType.DMA
    in_hbm = pl.BlockSpec(memory_space=pltpu.HBM)
    in_vmem = pl.BlockSpec(memory_space=pltpu.VMEM)
    in_smem = pl.BlockSpec(memory_space=pltpu.SMEM)
    out = pl.pallas_call(
        functools.partial(kernel, lines, inner, mps, heads, pairs),
        out_shape=jax.ShapeDtypeStruct((part_rows, width), bf16),
        in_specs=[in_hbm] * 4 + [in_smem] * 2 + [in_vmem] * 2,
        out_specs=in_hbm,
        scratch_shapes=[
            pltpu.VMEM((length, 1), jnp.int32),
            pltpu.VMEM((length // BLK, length), jnp.int32),
            pltpu.VMEM((lines, 2, slots, shard_rows, qkv_cols), bf16),
            pltpu.VMEM((lines, 2, slots, shard_rows, heads * HD), bf16),
            pltpu.VMEM((length, qkv_cols), f32),
            pltpu.VMEM((length, heads * HD), bf16),
            pltpu.VMEM((length, pairs * HD), bf16),
            pltpu.VMEM((length, pairs * HD), bf16),
            pltpu.VMEM((length, plane_cols), bf16),
            pltpu.VMEM((lines, mps - 1, part_rows, plane_cols), bf16),
            pltpu.VMEM((lines, mps - 1, part_rows, plane_cols), bf16),
            pltpu.VMEM((2, part_rows, plane_cols), bf16),
            dma((3,)),
            dma((2, 2, lines, 2)),
            dma((2, max(inner - 1, 1), lines, 2)),
            dma((2, 2, lines, max(inner - 1, 1))),
            dma((2, inner, lines, 2)),
            dma((2, lines, slots, 2)),
            dma((lines, mps - 1)),
            dma((lines, mps - 1)),
            dma((lines,)),
            dma((lines,)),
        ],
        compiler_params=pltpu.CompilerParams(
            collective_id=0, has_side_effects=True, vmem_limit_bytes=64 * 2**20 - 2**19
        ),
        cost_estimate=pl.CostEstimate(
            flops=4 * length * width * (qkv_cols + heads * HD) + 4 * length * length * heads * HD,
            bytes_accessed=4 * length * width,
            transcendentals=length * length * heads,
        ),
    )(states, q_weight, kv_weight, o_turned, modality, block_mask[0], cosine, sine)
    return out[None]


def solution(mesh):
    in_specs = (
        P("dp", None, None),
        P("dp", None),
        P("dp", None, None),
        P(None, "dp", "mp"),
        P(None, "dp", None),
        P(None, "mp", "dp"),
    )
    out_specs = P("dp", "mp", None)
    return jax.shard_map(
        functools.partial(local, mesh.shape["dp"], mesh.shape["mp"]),
        mesh=mesh, in_specs=in_specs, out_specs=out_specs, check_vma=False,
    )
```

```python
import functools
import math

import jax
import jax.numpy as jnp
import numpy as np
from jax import lax
from jax.experimental import pallas as pl
from jax.experimental.pallas import tpu as pltpu
from jax.sharding import PartitionSpec as P

HD = 128
KVH = 4
QHEADS = 16
BLK = 128
CORES = 2
MESH = pl.DeviceIdType.MESH
NT = (((1,), (1,)), ((), ()))


rope_theta = 1000000.0


def rotary_tables(length, head_width):
    half_width = head_width // 2
    frequency = rope_theta ** (-np.arange(half_width, dtype=np.float32) * 2.0 / head_width)
    angles = np.arange(length, dtype=np.float32)[:, None] * frequency.astype(np.float32)[None, :]
    sines = np.sin(angles)
    return (
        np.concatenate([np.cos(angles)] * 2, axis=1).astype(np.float32),
        np.concatenate([-sines, sines], axis=1).astype(np.float32),
    )


def split_chips(devices):
    chips = devices // CORES
    inner = 1 << (int(math.log2(chips)) // 2)
    return chips // inner, inner


def kernel(
    lines, inner, mps, heads, pairs,
    tok, in_q, in_kv, in_o, modality, block_mask, cosine, sine,
    out,
    kinds, layout, w_qkv, w_o, acc, queries, keys, values, tok_stage, send_buf, recv_buf, out_stage,
    load_sem, z_sem, x_sem, turn_sem, core_sem, recv_sem, y_send, y_recv, tok_sem, out_sem,
):
    length, width = tok.shape
    plane_cols = width // lines
    slots, shard_rows = w_qkv.shape[2], w_qkv.shape[3]
    part_rows = length // mps
    q_cols = heads * HD
    per_pair = heads // pairs
    row_tile = min(512, length)
    out_tile = min(256, part_rows)
    halves = part_rows // out_tile

    me = lax.axis_index("dp")
    mp = lax.axis_index("mp")
    core = me % CORES
    x = (me // CORES) % inner
    z = me // (CORES * inner)
    other = 1 - core
    mine = x * CORES + core

    def at(z_, x_, core_):
        return ((z_ * inner + x_) * CORES + core_, mp)

    def order(k):
        picked = jnp.int32(0)
        for place in range(lines):
            ranked = sorted(range(lines), key=lambda p: (abs(p - place), p))
            picked = jnp.where(z == place, ranked[k], picked)
        return picked

    weights = (w_qkv, w_o)

    def send(ph, p, s, m, sem, device):
        block = weights[ph].at[p, m, s]
        return pltpu.make_async_remote_copy(
            src_ref=block, dst_ref=block, send_sem=sem, recv_sem=recv_sem.at[ph, p, s, m],
            device_id=device, device_id_type=MESH,
        )

    def z_copies(ph, p, m):
        up = send(ph, p, mine, m, z_sem.at[ph, 0, p, m], at(z + 1, x, core))
        down = send(ph, p, mine, m, z_sem.at[ph, 1, p, m], at(z - 1, x, core))
        return ((p <= z) & (z < lines - 1), up), ((p >= z) & (z > 0), down)

    def push_z(ph, p, m):
        for condition, copy in z_copies(ph, p, m):
            pl.when(condition)(copy.start)

    def x_copy(ph, p, j, m):
        return send(ph, p, mine, m, x_sem.at[ph, j - 1, p, m], at(z, (x + j) % inner, core))

    def core_copy(ph, p, j, m):
        slot = ((x + j) % inner) * CORES + core
        return send(ph, p, slot, m, core_sem.at[ph, j, p, m], at(z, x, other))

    def ends(p):
        return (p == 0) | (p == lines - 1)

    def takes_x(p, m):
        return (p == z) | jnp.logical_not(ends(p)) if m == 0 else p >= 0

    def push_xc(ph, p, m):
        @pl.when(takes_x(p, m))
        def _():
            for j in range(1, inner):
                x_copy(ph, p, j, m).start()

        core_copy(ph, p, 0, m).start()

    def turn_copies(ph, p, j):
        slot = ((x + j) % inner) * CORES + core
        up = send(ph, p, slot, 0, turn_sem.at[ph, 0, p, j - 1], at(z + 1, x, core))
        down = send(ph, p, slot, 0, turn_sem.at[ph, 1, p, j - 1], at(z - 1, x, core))
        return ((p == 0) & (z < lines - 1), up), ((p == lines - 1) & (z > 0), down)

    def push_turn(ph, p, j):
        for condition, copy in turn_copies(ph, p, j):
            pl.when(condition)(copy.start)

    def turn(ph, distance):
        for valid, p in ((z == distance, 0), (z + distance == lines - 1, lines - 1)):
            @pl.when(valid)
            def _():
                for j in range(1, inner):
                    arrived(ph, p, ((x + j) % inner) * CORES + core, 0)
                    push_turn(ph, p, j)
                    core_copy(ph, p, j, 0).start()

    def arrived(ph, p, s, m):
        send(ph, p, s, m, core_sem.at[ph, 0, p, m], at(z, x, other)).wait_recv()

    def lane(ph, distance):
        for m in range(2):
            for valid, p in ((z >= distance, z - distance), (z + distance < lines, z + distance)):
                @pl.when(valid)
                def _():
                    arrived(ph, p, mine, m)
                    push_z(ph, p, m)
                    push_xc(ph, p, m)

    def complete(ph, p):
        for m in range(2):
            @pl.when(takes_x(p, m))
            def _():
                for j in range(1, inner):
                    arrived(ph, p, ((x + j) % inner) * CORES + core, m)
                    if m == 0:
                        pl.when(p == z)(lambda: push_turn(ph, p, j))
                    core_copy(ph, p, j, m).start()

        for m in range(2):
            for j in range(inner):
                arrived(ph, p, j * CORES + other, m)

    def token_copy(k):
        columns = pl.ds(pl.multiple_of(order(k) * plane_cols, 128), plane_cols)
        return pltpu.make_async_copy(tok.at[:, columns], tok_stage, tok_sem.at[k])

    def project(k):
        p = order(k)
        token_copy(k).wait()
        col_tile = min(512, w_qkv.shape[4])
        for c in range(0, w_qkv.shape[4], col_tile):
            @pl.loop(0, length // row_tile)
            def _(i):
                rows = pl.ds(pl.multiple_of(i * row_tile, row_tile), row_tile)
                block = tok_stage[rows, :]
                text = w_qkv[p, 0, :, :, c : c + col_tile].reshape(plane_cols, col_tile)
                image = w_qkv[p, 1, :, :, c : c + col_tile].reshape(plane_cols, col_tile)
                result = jnp.where(
                    kinds[rows, :] == 1,
                    jnp.dot(block, image, preferred_element_type=jnp.float32),
                    jnp.dot(block, text, preferred_element_type=jnp.float32),
                )
                if k == 0:
                    acc[rows, c : c + col_tile] = result
                else:
                    acc[rows, c : c + col_tile] += result
        if k + 1 < lines:
            token_copy(k + 1).start()

    def rope():
        tile = min(256, length)

        @pl.loop(0, length // tile)
        def _(i):
            rows = pl.ds(pl.multiple_of(i * tile, tile), tile)
            cos, sin = cosine[rows, :], sine[rows, :]

            def turned(first):
                part = acc[rows, first : first + HD]
                return (part * cos + pltpu.roll(part, HD // 2, 1) * sin).astype(jnp.bfloat16)

            for h in range(heads):
                queries[rows, h * HD : (h + 1) * HD] = turned(h * HD)
            for g in range(pairs):
                first = q_cols + g * 2 * HD
                keys[rows, g * HD : (g + 1) * HD] = turned(first)
                values[rows, g * HD : (g + 1) * HD] = acc[rows, first + HD : first + 2 * HD].astype(
                    jnp.bfloat16
                )

    def attend(part, start, stop):
        scale = HD ** (-0.5) * math.log2(math.e)
        together = 2 if per_pair % 2 == 0 else 1

        @pl.loop(start, stop)
        def _(i):
            block = part * (part_rows // BLK) + i
            rows = pl.ds(pl.multiple_of(block * BLK, BLK), BLK)
            seen = layout[pl.ds(block, 1), :]
            key_pos = lax.broadcasted_iota(jnp.int32, (BLK, length), 1)
            query_pos = lax.broadcasted_iota(jnp.int32, (BLK, length), 0) + block * BLK
            last = jnp.where(seen == 1, length, jnp.where(seen == 2, 0, -length))
            bias = jnp.where(key_pos <= query_pos + last, 0.0, -1e30)
            for g in range(pairs):
                key, value = keys[:, g * HD : (g + 1) * HD], values[:, g * HD : (g + 1) * HD]
                for first in range(g * per_pair, (g + 1) * per_pair, together):
                    query = jnp.concatenate(
                        [queries[rows, h * HD : (h + 1) * HD] for h in range(first, first + together)],
                        axis=0,
                    )
                    scores = lax.dot_general(query, key, NT, preferred_element_type=jnp.float32)
                    scores = scores.reshape(together, BLK, length) * scale + bias[None]
                    share = jnp.exp2(scores - jnp.max(scores, axis=-1, keepdims=True))
                    total = jnp.sum(share, axis=-1, keepdims=True)
                    mixed = jnp.dot(
                        share.astype(jnp.bfloat16).reshape(together * BLK, length),
                        value,
                        preferred_element_type=jnp.float32,
                    ).reshape(together, BLK, HD) / total
                    for h in range(together):
                        queries[rows, (first + h) * HD : (first + h + 1) * HD] = mixed[h].astype(
                            jnp.bfloat16
                        )

    def out_rows(p, first):
        rows = pl.ds(pl.multiple_of(first, out_tile), out_tile)
        block = queries[rows, :]
        text = w_o[p, 0].reshape(plane_cols, q_cols)
        image = w_o[p, 1].reshape(plane_cols, q_cols)
        result = jnp.where(
            kinds[rows, :] == 1,
            lax.dot_general(block, image, NT, preferred_element_type=jnp.float32),
            lax.dot_general(block, text, NT, preferred_element_type=jnp.float32),
        )
        return result.astype(jnp.bfloat16)

    def y_copy(k, j, h):
        rows = pl.ds(h * out_tile, out_tile)
        return pltpu.make_async_remote_copy(
            src_ref=send_buf.at[k, j - 1, rows], dst_ref=recv_buf.at[k, j - 1, rows],
            send_sem=y_send.at[k, j - 1, h], recv_sem=y_recv.at[k, j - 1, h],
            device_id=(me, (mp + j) % mps), device_id_type=MESH,
        )

    def give(k, h):
        for j in range(1, mps):
            first = ((mp + j) % mps) * part_rows + h * out_tile
            send_buf[k, j - 1, h * out_tile : (h + 1) * out_tile, :] = out_rows(order(k), first)
            y_copy(k, j, h).start()

    def out_copy(k):
        columns = pl.ds(pl.multiple_of(order(k) * plane_cols, 128), plane_cols)
        return pltpu.make_async_copy(out_stage.at[k % 2], out.at[:, columns], out_sem.at[k])

    def take(k):
        if k >= 2:
            out_copy(k - 2).wait()
        for h in range(halves):
            rows = slice(h * out_tile, (h + 1) * out_tile)
            out_stage[k % 2, rows, :] = out_rows(order(k), mp * part_rows + h * out_tile)
        for h in range(halves):
            rows = slice(h * out_tile, (h + 1) * out_tile)
            total = out_stage[k % 2, rows, :].astype(jnp.float32)
            for j in range(1, mps):
                y_copy(k, j, h).wait_recv()
                total += recv_buf[k, j - 1, rows, :].astype(jnp.float32)
            out_stage[k % 2, rows, :] = total.astype(jnp.bfloat16)
        out_copy(k).start()

    pair_cols = pairs * 2 * HD
    first_pair = (mp * heads // (QHEADS // KVH)) * (2 * HD)
    kv_part = in_kv.at[:, :, pl.ds(pl.multiple_of(first_pair, 2 * HD), pair_cols)]
    loads = [
        pltpu.make_async_copy(in_q, w_qkv.at[z, :, mine, :, pl.ds(0, q_cols)], load_sem.at[0]),
        pltpu.make_async_copy(kv_part, w_qkv.at[z, :, mine, :, pl.ds(q_cols, pair_cols)], load_sem.at[1]),
        pltpu.make_async_copy(in_o, w_o.at[z, :, mine], load_sem.at[2]),
    ]
    for load in loads:
        load.start()
    token_copy(0).start()

    barrier = pltpu.get_barrier_semaphore()

    def greet(device):
        pl.semaphore_signal(barrier, inc=1, device_id=device, device_id_type=MESH)

    pl.when(z > 0)(lambda: greet(at(z - 1, x, core)))
    pl.when(z < lines - 1)(lambda: greet(at(z + 1, x, core)))
    for j in range(1, inner):
        greet(at(z, (x + j) % inner, core))
    greet(at(z, x, other))
    for j in range(1, mps):
        greet((me, (mp + j) % mps))
    along = jnp.where(z > 0, 1, 0) + jnp.where(z < lines - 1, 1, 0)
    pl.semaphore_wait(barrier, inner + mps - 1 + along)

    loads[0].wait()
    loads[1].wait()
    for m in range(2):
        push_z(0, z, m)
        push_xc(0, z, m)
    loads[2].wait()
    blocks = length // BLK
    for i in range(blocks):
        kinds[i * BLK : (i + 1) * BLK, :] = jnp.full((BLK, 1), modality[0, i], jnp.int32)
        for j in range(blocks):
            layout[i : i + 1, j * BLK : (j + 1) * BLK] = jnp.full((1, BLK), block_mask[i, j], jnp.int32)
    for k in range(lines):
        if k > 0:
            turn(0, k)
        if k + 1 < lines:
            lane(0, k + 1)
        if k == max(lines - 2, 0):
            for m in range(2):
                push_z(1, z, m)
        complete(0, order(k))
        if k == lines - 1:
            for m in range(2):
                push_xc(1, z, m)
        project(k)
    if lines > 1:
        lane(1, 1)
    rope()
    part_blocks = part_rows // BLK
    tile_blocks = out_tile // BLK
    for h in range(halves):
        for j in range(1, mps):
            attend((mp + j) % mps, h * tile_blocks, (h + 1) * tile_blocks)
        if h == 0:
            complete(1, order(0))
        give(0, h)
        if h == 0 and lines > 2:
            lane(1, 2)
    attend(mp, 0, part_blocks // 2)
    if lines > 1:
        turn(1, 1)
    attend(mp, part_blocks // 2, part_blocks)
    for k in range(1, lines):
        if k > 1:
            turn(1, k)
        if k + 2 <= lines - 1:
            lane(1, k + 2)
        complete(1, order(k))
        for h in range(halves):
            give(k, h)
        take(k - 1)
    take(lines - 1)

    for k in range(max(lines - 2, 0), lines):
        out_copy(k).wait()
    for k in range(lines):
        for j in range(1, mps):
            for h in range(halves):
                y_copy(k, j, h).wait_send()
    for ph in range(2):
        for p in range(lines):
            for m in range(2):
                for condition, copy in z_copies(ph, p, m):
                    pl.when(condition)(copy.wait_send)
                @pl.when(takes_x(p, m))
                def _():
                    for j in range(1, inner):
                        x_copy(ph, p, j, m).wait_send()

                for j in range(inner):
                    core_copy(ph, p, j, m).wait_send()
            if p in (0, lines - 1):
                for j in range(1, inner):
                    for condition, copy in turn_copies(ph, p, j):
                        pl.when(condition)(copy.wait_send)


def local(devices, mps, tokens, modality, block_mask, q_weight, kv_weight, o_weight):
    states = tokens[0]
    length, width = states.shape
    heads = q_weight.shape[2] // HD
    group_size = QHEADS // KVH
    pairs = max(1, heads // group_size)
    o_turned = jnp.swapaxes(o_weight, 1, 2)
    cosine, sine = rotary_tables(length, HD)

    lines, inner = split_chips(devices)
    slots = inner * CORES
    plane_cols = width // lines
    part_rows = length // mps
    shard_rows, qkv_cols = q_weight.shape[1], (heads + 2 * pairs) * HD
    bf16, f32 = jnp.bfloat16, jnp.float32
    dma = pltpu.SemaphoreType.DMA
    in_hbm = pl.BlockSpec(memory_space=pltpu.HBM)
    in_vmem = pl.BlockSpec(memory_space=pltpu.VMEM)
    in_smem = pl.BlockSpec(memory_space=pltpu.SMEM)
    out = pl.pallas_call(
        functools.partial(kernel, lines, inner, mps, heads, pairs),
        out_shape=jax.ShapeDtypeStruct((part_rows, width), bf16),
        in_specs=[in_hbm] * 4 + [in_smem] * 2 + [in_vmem] * 2,
        out_specs=in_hbm,
        scratch_shapes=[
            pltpu.VMEM((length, 1), jnp.int32),
            pltpu.VMEM((length // BLK, length), jnp.int32),
            pltpu.VMEM((lines, 2, slots, shard_rows, qkv_cols), bf16),
            pltpu.VMEM((lines, 2, slots, shard_rows, heads * HD), bf16),
            pltpu.VMEM((length, qkv_cols), f32),
            pltpu.VMEM((length, heads * HD), bf16),
            pltpu.VMEM((length, pairs * HD), bf16),
            pltpu.VMEM((length, pairs * HD), bf16),
            pltpu.VMEM((length, plane_cols), bf16),
            pltpu.VMEM((lines, mps - 1, part_rows, plane_cols), bf16),
            pltpu.VMEM((lines, mps - 1, part_rows, plane_cols), bf16),
            pltpu.VMEM((2, part_rows, plane_cols), bf16),
            dma((3,)),
            dma((2, 2, lines, 2)),
            dma((2, max(inner - 1, 1), lines, 2)),
            dma((2, 2, lines, max(inner - 1, 1))),
            dma((2, inner, lines, 2)),
            dma((2, lines, slots, 2)),
            dma((lines, mps - 1, max(part_rows // 256, 1))),
            dma((lines, mps - 1, max(part_rows // 256, 1))),
            dma((lines,)),
            dma((lines,)),
        ],
        compiler_params=pltpu.CompilerParams(
            collective_id=0, has_side_effects=True, vmem_limit_bytes=64 * 2**20 - 2**19
        ),
        cost_estimate=pl.CostEstimate(
            flops=4 * length * width * (qkv_cols + heads * HD) + 4 * length * length * heads * HD,
            bytes_accessed=4 * length * width,
            transcendentals=length * length * heads,
        ),
    )(states, q_weight, kv_weight, o_turned, modality, block_mask[0], cosine, sine)
    return out[None]


def solution(mesh):
    in_specs = (
        P("dp", None, None),
        P("dp", None),
        P("dp", None, None),
        P(None, "dp", "mp"),
        P(None, "dp", None),
        P(None, "mp", "dp"),
    )
    out_specs = P("dp", "mp", None)
    return jax.shard_map(
        functools.partial(local, mesh.shape["dp"], mesh.shape["mp"]),
        mesh=mesh, in_specs=in_specs, out_specs=out_specs, check_vma=False,
    )
```
